256 devices in a mesh: row: 32 (over z_lo, x, core), col: 8 (over z_hi, y).
Axes of the slice: x: 4, y: 4, z: 8 (z_hi: 2, z_lo: 4; z = z_hi * 4 + z_lo), core: 2. Of those that a mesh axis runs over, the one named last changes fastest.
Arguments:
- tokens: bfloat16 [768, 8192], P('row', 'col'), may hold values from -6 to 6
- gate_weight: bfloat16 [8192, 16384], P('col', 'row'), may hold values from -0.0625 to 0.0625
- up_weight: bfloat16 [8192, 16384], P('col', 'row'), may hold values from -0.0625 to 0.0625
- down_weight: bfloat16 [16384, 8192], P('row', 'col'), may hold values from -0.046875 to 0.046875
- cotangent: bfloat16 [768, 8192], P('row', 'col'), may hold values from -0.59765625 to 0.59765625
Outputs:
- output: bfloat16 [768, 8192], P('row', 'col')
- grad_tokens: bfloat16 [768, 8192], P('row', 'col')
- grad_gate: bfloat16 [8192, 16384], P('col', 'row')
- grad_up: bfloat16 [8192, 16384], P('col', 'row')
- grad_down: bfloat16 [16384, 8192], P('row', 'col')
The draws below stay inside these ranges and needn't reach their ends.
All inputs are finite; a program needn't handle non-finite values.
Results may differ from the reference program's by a relative error of at most 0.005.
Values may be sent and summed in bfloat16 or wider, within the bound.
No kernel may reach another device: no remote copies, remote signals or barrier semaphores. Data moves between devices by JAX's collectives and lax.ppermute only.
A program may use at most 64 MiB of HBM per device.

```python
import jax
import jax.numpy as jnp

D = 8192
FF = 16384
TOKENS = 768


def level_of(rng, extent, cuts, least, high):
    loudness = 1.0
    for axis_at, parts in cuts:
        draws = jax.random.uniform(jax.random.fold_in(jax.random.fold_in(rng, 6), axis_at), (parts,), jnp.float32, least / len(cuts), high / len(cuts))
        loudness = loudness * jnp.repeat(jnp.exp(draws), extent[axis_at] // parts).reshape((-1,) + (1,) * (len(extent) - 1 - axis_at))
    return loudness


def bell_draw(own_key, shape, width, limit, split=(), kind=jnp.bfloat16):
    result = width * jax.random.normal(own_key, shape, jnp.float32)
    if split:
        result = result * level_of(own_key, shape, split, -0.22, 0.18)
    return jnp.clip(result, -limit, limit).astype(kind)


def setup_inputs(seed: int = 0) -> dict:
    arg_keys = jax.random.split(jax.random.key(seed), 6)
    tokens = bell_draw(arg_keys[0], (TOKENS, D), 1.0, 6.0, ((0, 32), (1, 8)))
    gate_weight = bell_draw(arg_keys[1], (D, FF), D ** -0.5, 0.0625, ((0, 8), (1, 32)))
    up_weight = bell_draw(arg_keys[2], (D, FF), D ** -0.5, 0.0625, ((0, 8), (1, 32)))
    down_weight = bell_draw(arg_keys[3], (FF, D), FF ** -0.5, 0.046875, ((0, 32), (1, 8)))
    cotangent = bell_draw(arg_keys[4], (TOKENS, D), 0.1, 0.59765625, ((0, 32), (1, 8)))
    return dict(tokens=tokens, gate_weight=gate_weight, up_weight=up_weight, down_weight=down_weight, cotangent=cotangent)


def reference(tokens, gate_weight, up_weight, down_weight, cotangent):
    gate = jnp.dot(tokens, gate_weight, preferred_element_type=jnp.float32)
    up = jnp.dot(tokens, up_weight, preferred_element_type=jnp.float32)
    sig = jax.nn.sigmoid(gate)
    hidden = (gate * sig * up).astype(jnp.bfloat16)
    output = jnp.dot(hidden, down_weight, preferred_element_type=jnp.float32).astype(jnp.bfloat16)
    grad_hidden = jnp.dot(cotangent, down_weight.T, preferred_element_type=jnp.float32)
    grad_gate_act = (grad_hidden * up * sig * (1.0 + gate * (1.0 - sig))).astype(jnp.bfloat16)
    grad_up_act = (grad_hidden * gate * sig).astype(jnp.bfloat16)
    grad_down = jnp.dot(hidden.T, cotangent, preferred_element_type=jnp.float32).astype(jnp.bfloat16)
    grad_gate = jnp.dot(tokens.T, grad_gate_act, preferred_element_type=jnp.float32).astype(jnp.bfloat16)
    grad_up = jnp.dot(tokens.T, grad_up_act, preferred_element_type=jnp.float32).astype(jnp.bfloat16)
    grad_tokens = (jnp.dot(grad_gate_act, gate_weight.T, preferred_element_type=jnp.float32)
                   + jnp.dot(grad_up_act, up_weight.T, preferred_element_type=jnp.float32)).astype(jnp.bfloat16)
    return (output, grad_tokens, grad_gate, grad_up, grad_down)
```

```python
import jax
import jax.numpy as jnp
from jax import lax
from jax.sharding import PartitionSpec as P

Z, X, CORES, ZH, Y = 4, 4, 2, 2, 4
BF = jnp.bfloat16
F32 = jnp.float32


def row_perm(move):
    pairs = []
    for z in range(Z):
        for x in range(X):
            for c in range(CORES):
                tz, tx, tc = move(z, x, c)
                pairs.append(
                    ((z * X + x) * CORES + c, ((tz % Z) * X + tx % X) * CORES + tc % CORES)
                )
    return pairs


def col_perm(move):
    pairs = []
    for h in range(ZH):
        for y in range(Y):
            th, ty = move(h, y)
            pairs.append((h * Y + y, (th % ZH) * Y + ty % Y))
    return pairs


def send_z(a, k):
    return lax.ppermute(a, "row", row_perm(lambda z, x, c: (z + k, x, c)))


def send_x(a, k):
    return lax.ppermute(a, "row", row_perm(lambda z, x, c: (z, x + k, c)))


def send_core(a):
    return lax.ppermute(a, "row", row_perm(lambda z, x, c: (z, x, c + 1)))


def send_y(a, k):
    return lax.ppermute(a, "col", col_perm(lambda h, y: (h, y + k)))


def send_half(a):
    return lax.ppermute(a, "col", col_perm(lambda h, y: (h + 1, y)))


def dot(left, right, ldim, rdim):
    return lax.dot_general(
        left, right, (((ldim,), (rdim,)), ((), ())), preferred_element_type=F32
    )


def gather_row(a):
    a = jnp.concatenate([a] + [send_z(a, k) for k in range(1, Z)], axis=0)
    a = jnp.concatenate([a] + [send_x(a, k) for k in range(1, X)], axis=0)
    return jnp.concatenate([a, send_core(a)], axis=0)


def scatter_row(part, rows):
    half = rows // CORES
    theirs = send_core(part(half, half).astype(BF))
    total = part(0, half) + theirs.astype(F32)
    for count, send in ((X, send_x), (Z, send_z)):
        size = total.shape[0] // count
        pieces = [
            send(total[k * size : (k + 1) * size].astype(BF), -k) for k in range(1, count)
        ]
        total = total[:size]
        for piece in pieces:
            total = total + piece.astype(F32)
    return total.astype(BF)


def scatter_col(part):
    y = lax.axis_index("col") % Y
    pieces = [send_y(part((y + k) % Y).astype(BF), k) for k in range(1, Y)]
    total = part(y)
    for piece in pieces:
        total = total + piece.astype(F32)
    return total + send_half(total.astype(BF)).astype(F32)


def gather_col(a):
    y = lax.axis_index("col") % Y
    size = a.shape[0]
    out = jnp.zeros((size * Y,) + a.shape[1:], a.dtype)
    for k in range(Y):
        piece = send_y(a, k) if k else a
        out = lax.dynamic_update_slice_in_dim(out, piece, ((y - k) % Y) * size, axis=0)
    return out


def on_device(tokens, gate_weight, up_weight, down_weight, cotangent):
    all_tokens = gather_row(tokens)
    all_cotangent = gather_row(cotangent)
    block = all_tokens.shape[0] // Y

    def rows(a, at):
        return lax.dynamic_slice_in_dim(a, at * block, block, axis=0)

    def gate_up_part(at):
        piece = rows(all_tokens, at)
        return jnp.concatenate(
            [dot(piece, gate_weight, 1, 0), dot(piece, up_weight, 1, 0)], axis=1
        )

    gate_up = scatter_col(gate_up_part)
    width = gate_weight.shape[1]
    gate, up = gate_up[:, :width], gate_up[:, width:]
    grad_hidden = scatter_col(lambda at: dot(rows(all_cotangent, at), down_weight, 1, 1))

    sig = jax.nn.sigmoid(gate)
    hidden = (gate * sig * up).astype(BF)
    all_hidden = gather_col(hidden)
    output = scatter_row(
        lambda at, size: dot(all_hidden[at : at + size], down_weight, 1, 0),
        all_hidden.shape[0],
    )
    grad_down = dot(all_hidden, all_cotangent, 0, 0).astype(BF)

    gate_grad = (grad_hidden * up * sig * (1.0 + gate * (1.0 - sig))).astype(BF)
    up_grad = (grad_hidden * gate * sig).astype(BF)
    all_grads = gather_col(jnp.concatenate([gate_grad, up_grad], axis=1))
    all_gate_grad, all_up_grad = all_grads[:, :width], all_grads[:, width:]
    grad_tokens = scatter_row(
        lambda at, size: dot(all_gate_grad[at : at + size], gate_weight, 1, 1)
        + dot(all_up_grad[at : at + size], up_weight, 1, 1),
        all_grads.shape[0],
    )
    grad_gate = dot(all_tokens, all_gate_grad, 0, 0).astype(BF)
    grad_up = dot(all_tokens, all_up_grad, 0, 0).astype(BF)
    return (output, grad_tokens, grad_gate, grad_up, grad_down)


def solution(mesh):
    return jax.shard_map(
        on_device,
        mesh=mesh,
        in_specs=(
            P("row", "col"),
            P("col", "row"),
            P("col", "row"),
            P("row", "col"),
            P("row", "col"),
        ),
        out_specs=(
            P("row", "col"),
            P("row", "col"),
            P("col", "row"),
            P("col", "row"),
            P("row", "col"),
        ),
        check_vma=False,
    )
```

```python
import jax
import jax.numpy as jnp
from jax import lax
from jax.experimental import pallas as pl
from jax.experimental.pallas import tpu as pltpu
from jax.sharding import PartitionSpec as P

Z, X, CORES, ZH, Y = 4, 4, 2, 2, 4
BF = jnp.bfloat16
F32 = jnp.float32
VMEM_LIMIT = 32 * 1024 * 1024


def row_perm(move):
    pairs = []
    for z in range(Z):
        for x in range(X):
            for c in range(CORES):
                tz, tx, tc = move(z, x, c)
                pairs.append(
                    ((z * X + x) * CORES + c, ((tz % Z) * X + tx % X) * CORES + tc % CORES)
                )
    return pairs


def col_perm(move):
    pairs = []
    for h in range(ZH):
        for y in range(Y):
            th, ty = move(h, y)
            pairs.append((h * Y + y, (th % ZH) * Y + ty % Y))
    return pairs


def send_z(a, k):
    return lax.ppermute(a, "row", row_perm(lambda z, x, c: (z + k, x, c)))


def send_x(a, k):
    return lax.ppermute(a, "row", row_perm(lambda z, x, c: (z, x + k, c)))


def send_core(a):
    return lax.ppermute(a, "row", row_perm(lambda z, x, c: (z, x, c + 1)))


def send_y(a, k):
    return lax.ppermute(a, "col", col_perm(lambda h, y: (h, y + k)))


def send_half(a):
    return lax.ppermute(a, "col", col_perm(lambda h, y: (h + 1, y)))


def dot(left, right, ldim, rdim):
    return lax.dot_general(
        left, right, (((ldim,), (rdim,)), ((), ())), preferred_element_type=F32
    )


def call(kernel, outs, args, flops=0, scalar=None, after=()):
    out_shape = [jax.ShapeDtypeStruct(s, d) for s, d in outs]
    moved = sum(a.size * a.dtype.itemsize for a in args)
    moved += sum(o.size * o.dtype.itemsize for o in out_shape)
    vmem = pl.BlockSpec(memory_space=pltpu.VMEM)
    in_specs = [vmem] * len(args)
    if scalar is not None:
        in_specs = [pl.BlockSpec(memory_space=pltpu.SMEM)] + in_specs
        args = [scalar, *args]
    n = len(args)
    body = kernel
    if after:
        in_specs = in_specs + [pl.BlockSpec(memory_space=pl.ANY)] * len(after)
        args = [*args, *after]

        def body(*refs):
            kernel(*refs[:n], *refs[n + len(after) :])

    return pl.pallas_call(
        body,
        out_shape=out_shape,
        in_specs=in_specs,
        out_specs=[vmem] * len(outs),
        compiler_params=pltpu.CompilerParams(vmem_limit_bytes=VMEM_LIMIT),
        cost_estimate=pl.CostEstimate(
            flops=flops, bytes_accessed=moved, transcendentals=0
        ),
    )(*args)


def block_at(index, size):
    return pl.ds(pl.multiple_of(lax.rem(index, Y) * size, size), size)


def cat_z_kernel(a, b, c, d, out):
    parts = [r[...].astype(F32) for r in (a, b, c, d)]
    out[...] = jnp.concatenate(parts, axis=0).astype(BF)


def cat_x_kernel(a, b, c, d, out):
    size = a.shape[0]
    for k, r in enumerate((a, b, c, d)):
        out[k * size : (k + 1) * size] = r[...]


def hold_kernel(*refs):
    half = len(refs) // 2
    for src, dst in zip(refs[:half], refs[half:]):
        dst[...] = src[...]


def hold(args, after):
    return call(hold_kernel, [(a.shape, a.dtype) for a in args], list(args), after=after)


def gather_z(a):
    n, w = a.shape
    parts = [a] + [send_z(a, k) for k in (2, 1, 3)]
    a, c, b, d = parts
    return call(cat_z_kernel, [((Z * n, w), BF)], [a, b, c, d])[0]


def gather_x(a, got, after=()):
    n, w = a.shape
    return call(cat_x_kernel, [((X * n, w), BF)], [a, *got], after=after)[0]


def all_x(a):
    c, b, d = [send_x(a, k) for k in (2, 1, 3)]
    return [b, c, d]


def all_y(sends):
    c, b, d = [send_y(sends[k - 1], k) for k in (2, 1, 3)]
    return [b, c, d]


def up_kernel(y, mine, theirs, wg, wu, whole, s1, s2, s3, own):
    half = mine.shape[0]
    whole[:half] = mine[...]
    whole[half:] = theirs[...]
    n, f = s1.shape[0], wg.shape[1]
    for k, o in ((1, s1), (2, s2), (3, s3), (0, own)):
        rows = whole[block_at(y[0] + k, n), :]
        o[:, :f] = dot(rows, wg[...], 1, 0).astype(o.dtype)
        o[:, f:] = dot(rows, wu[...], 1, 0).astype(o.dtype)


def back_kernel(y, mine, theirs, wd, whole, s1, s2, s3, own):
    half = mine.shape[0]
    whole[:half] = mine[...]
    whole[half:] = theirs[...]
    n = s1.shape[0]
    for k, o in ((1, s1), (2, s2), (3, s3), (0, own)):
        rows = whole[block_at(y[0] + k, n), :]
        o[...] = dot(rows, wd[...], 1, 1).astype(o.dtype)


def sum_y_kernel(own, a, b, c, total, send):
    t = own[...] + a[...].astype(F32) + b[...].astype(F32) + c[...].astype(F32)
    total[...] = t
    send[...] = t.astype(BF)


def hidden_kernel(mine, theirs, out):
    f = out.shape[1]
    gate = mine[:, :f] + theirs[:, :f].astype(F32)
    up = mine[:, f:] + theirs[:, f:].astype(F32)
    out[...] = (gate * jax.nn.sigmoid(gate) * up).astype(BF)


def grads_kernel(mine, theirs, mine_h, theirs_h, out):
    f = mine_h.shape[1]
    gate = mine[:, :f] + theirs[:, :f].astype(F32)
    up = mine[:, f:] + theirs[:, f:].astype(F32)
    gh = mine_h[...] + theirs_h[...].astype(F32)
    sig = jax.nn.sigmoid(gate)
    out[:, :f] = (gh * up * sig * (1.0 + gate * (1.0 - sig))).astype(BF)
    out[:, f:] = (gh * gate * sig).astype(BF)


def place(y, parts, whole):
    n = parts[0].shape[0]
    for k, r in enumerate(parts):
        whole[block_at(y[0] + Y - k, n), :] = r[...]


def out_kernel(y, a, b, c, d, wd, whole, own, theirs):
    place(y, (a, b, c, d), whole)
    half = own.shape[0]
    theirs[...] = dot(whole[half:, :], wd[...], 1, 0).astype(theirs.dtype)
    own[...] = dot(whole[:half, :], wd[...], 1, 0)


def tokens_kernel(y, a, b, c, d, wg, wu, gg, ug, own, theirs):
    f = gg.shape[1]
    n = a.shape[0]
    for k, r in enumerate((a, b, c, d)):
        at = block_at(y[0] + Y - k, n)
        gg[at, :] = r[:, :f]
        ug[at, :] = r[:, f:]
    half = own.shape[0]
    for o, at in ((theirs, slice(half, None)), (own, slice(0, half))):
        t = dot(gg[at, :], wg[...], 1, 1) + dot(ug[at, :], wu[...], 1, 1)
        o[...] = t.astype(o.dtype)


def rs_first_kernel(mine, theirs, s1, s2, s3, own):
    n = own.shape[0]
    for k, o in enumerate((own, s1, s2, s3)):
        at = slice(k * n, (k + 1) * n)
        o[...] = (mine[at, :] + theirs[at, :].astype(F32)).astype(o.dtype)


def rs_next_kernel(mine, a, b, c, s1, s2, s3, own):
    n = own.shape[0]
    t = mine[...] + a[...].astype(F32) + b[...].astype(F32) + c[...].astype(F32)
    for k, o in enumerate((own, s1, s2, s3)):
        o[...] = t[k * n : (k + 1) * n].astype(o.dtype)


def rs_last_kernel(mine, a, b, c, out):
    t = mine[...] + a[...].astype(F32) + b[...].astype(F32) + c[...].astype(F32)
    out[...] = t.astype(BF)


def first_row(own, theirs, after=()):
    rows, w = own.shape
    sends = [((rows // X, w), BF)] * 3 + [((rows // X, w), F32)]
    return call(rs_first_kernel, sends, [own, theirs], after=after)


def back_x(sends):
    c, b, d = [send_x(sends[k - 1], -k) for k in (2, 1, 3)]
    return [b, c, d]


def next_row(own, got, after=()):
    rows, w = own.shape
    sends = [((rows // Z, w), BF)] * 3 + [((rows // Z, w), F32)]
    return call(rs_next_kernel, sends, [own, *got], after=after)


def back_z(sends):
    c, b, d = [send_z(sends[k - 1], -k) for k in (2, 1, 3)]
    return [b, c, d]


def last_row(own, got):
    return call(rs_last_kernel, [(own.shape, BF)], [own, *got])[0]


def on_device(tokens, gate_weight, up_weight, down_weight, cotangent):
    y = lax.rem(lax.axis_index("col"), Y).astype(jnp.int32).reshape(1)
    d, f = gate_weight.shape

    t = gather_z(tokens)
    g = gather_z(hold([cotangent], [t])[0])
    t = gather_x(t, all_x(t), after=[g])
    half = t.shape[0]
    n = CORES * half // Y
    flops = 2 * CORES * half * d * f

    def sends(w):
        return [((CORES * half, d), BF)] + [((n, w), BF)] * 3 + [((n, w), F32)]

    all_tokens, s1, s2, s3, own = call(
        up_kernel, sends(2 * f), [t, send_core(t), gate_weight, up_weight], 2 * flops, y
    )
    g = hold([g], [s1])[0]
    got_x = all_x(g)
    got = all_y([s1, s2, s3])
    g = gather_x(g, got_x, after=got)
    gate_up, part = call(
        sum_y_kernel, [((n, 2 * f), F32), ((n, 2 * f), BF)], [own, *got], after=got_x
    )

    gate_up2 = send_half(part)
    all_cotangent, s1, s2, s3, own = call(
        back_kernel, sends(f), [g, send_core(g), down_weight], flops, y
    )
    got = all_y([s1, s2, s3])
    gh, part = call(
        sum_y_kernel, [((n, f), F32), ((n, f), BF)], [own, *got], after=[gate_up2]
    )
    hidden = call(hidden_kernel, [((n, f), BF)], [gate_up, gate_up2], after=got)[0]

    gh2 = send_half(part)
    got = all_y([hidden] * 3)
    all_hidden, own_out, their_out = call(
        out_kernel,
        [((Y * n, f), BF), ((half, d), F32), ((half, d), OUT_CORE)],
        [hidden, *got, down_weight],
        flops,
        y,
        after=[gh2],
    )
    grads = call(
        grads_kernel, [((n, 2 * f), BF)], [gate_up, gate_up2, gh, gh2], after=got
    )[0]

    s1, s2, s3, own_out = first_row(own_out, send_core(their_out))
    got_out = back_x([s1, s2, s3])
    got = all_y([grads] * 3)
    gg, ug, own_gt, their_gt = call(
        tokens_kernel,
        [((Y * n, f), BF), ((Y * n, f), BF), ((half, d), F32), ((half, d), OUT_CORE)],
        [grads, *got, gate_weight, up_weight],
        2 * flops,
        y,
        after=got_out,
    )
    s1, s2, s3, own_out = next_row(own_out, got_out, after=got)
    z_out = [s1, s2, s3]
    s1, s2, s3, own_gt = first_row(own_gt, send_core(their_gt))
    z_out = hold(z_out, [s1])
    got_z = back_z(z_out)
    got = back_x([s1, s2, s3])
    output = last_row(own_out, got_z)
    grad_down = dot(all_hidden, all_cotangent, 0, 0).astype(BF)
    s1, s2, s3, own_gt = next_row(own_gt, got, after=got_z)
    grad_tokens = last_row(own_gt, back_z([s1, s2, s3]))
    grad_gate = dot(all_tokens, gg, 0, 0).astype(BF)
    grad_up = dot(all_tokens, ug, 0, 0).astype(BF)
    return (output, grad_tokens, grad_gate, grad_up, grad_down)


OUT_CORE = F32


def solution(mesh):
    return jax.shard_map(
        on_device,
        mesh=mesh,
        in_specs=(
            P("row", "col"),
            P("col", "row"),
            P("col", "row"),
            P("row", "col"),
            P("row", "col"),
        ),
        out_specs=(
            P("row", "col"),
            P("row", "col"),
            P("col", "row"),
            P("col", "row"),
            P("row", "col"),
        ),
        check_vma=False,
    )
```

```python
import jax
import jax.numpy as jnp
from jax import lax
from jax.experimental import pallas as pl
from jax.experimental.pallas import tpu as pltpu
from jax.sharding import PartitionSpec as P

Z, X, CORES, ZH, Y = 4, 4, 2, 2, 4
BF = jnp.bfloat16
F32 = jnp.float32
VMEM_LIMIT = 32 * 1024 * 1024


def row_perm(move):
    pairs = []
    for z in range(Z):
        for x in range(X):
            for c in range(CORES):
                tz, tx, tc = move(z, x, c)
                pairs.append(
                    ((z * X + x) * CORES + c, ((tz % Z) * X + tx % X) * CORES + tc % CORES)
                )
    return pairs


def col_perm(move):
    pairs = []
    for h in range(ZH):
        for y in range(Y):
            th, ty = move(h, y)
            pairs.append((h * Y + y, (th % ZH) * Y + ty % Y))
    return pairs


def send_z(a, k, name):
    with jax.named_scope(name):
        return lax.ppermute(a, "row", row_perm(lambda z, x, c: (z + k, x, c)))


def send_x(a, k, name):
    with jax.named_scope(name):
        return lax.ppermute(a, "row", row_perm(lambda z, x, c: (z, x + k, c)))


def send_core(a, name):
    with jax.named_scope(name):
        return lax.ppermute(a, "row", row_perm(lambda z, x, c: (z, x, c + 1)))


def send_y(a, k, name):
    with jax.named_scope(name):
        return lax.ppermute(a, "col", col_perm(lambda h, y: (h, y + k)))


def send_half(a, name):
    with jax.named_scope(name):
        return lax.ppermute(a, "col", col_perm(lambda h, y: (h + 1, y)))


def dot(left, right, ldim, rdim):
    return lax.dot_general(
        left, right, (((ldim,), (rdim,)), ((), ())), preferred_element_type=F32
    )


def call(kernel, outs, args, flops=0, scalar=None, after=()):
    out_shape = [jax.ShapeDtypeStruct(s, d) for s, d in outs]
    moved = sum(a.size * a.dtype.itemsize for a in args)
    moved += sum(o.size * o.dtype.itemsize for o in out_shape)
    vmem = pl.BlockSpec(memory_space=pltpu.VMEM)
    in_specs = [vmem] * len(args)
    if scalar is not None:
        in_specs = [pl.BlockSpec(memory_space=pltpu.SMEM)] + in_specs
        args = [scalar, *args]
    n = len(args)
    body = kernel
    if after:
        in_specs = in_specs + [pl.BlockSpec(memory_space=pl.ANY)] * len(after)
        args = [*args, *after]

        def body(*refs):
            kernel(*refs[:n], *refs[n + len(after) :])

    return pl.pallas_call(
        body,
        name=kernel.__name__.removesuffix("_kernel"),
        out_shape=out_shape,
        in_specs=in_specs,
        out_specs=[vmem] * len(outs),
        compiler_params=pltpu.CompilerParams(vmem_limit_bytes=VMEM_LIMIT),
        cost_estimate=pl.CostEstimate(
            flops=flops, bytes_accessed=moved, transcendentals=0
        ),
    )(*args)


def block_at(index, size):
    return pl.ds(pl.multiple_of(lax.rem(index, Y) * size, size), size)


def cat_z_kernel(a, b, c, d, out):
    parts = [r[...].astype(F32) for r in (a, b, c, d)]
    out[...] = jnp.concatenate(parts, axis=0).astype(BF)


def cat_x_kernel(a, b, c, d, out):
    size = a.shape[0]
    for k, r in enumerate((a, b, c, d)):
        out[k * size : (k + 1) * size] = r[...]


def hold_kernel(*refs):
    half = len(refs) // 2
    for src, dst in zip(refs[:half], refs[half:]):
        dst[...] = src[...]


def hold(args, after):
    return call(hold_kernel, [(a.shape, a.dtype) for a in args], list(args), after=after)


def gather_z(a, got):
    n, w = a.shape
    own = hold([a], [])[0]
    return call(cat_z_kernel, [((Z * n, w), BF)], [own, *got])[0]


def gather_x(a, got, after=()):
    n, w = a.shape
    return call(cat_x_kernel, [((X * n, w), BF)], [a, *got], after=after)[0]


def by_distance(send, sends, name, sign=1):
    c, b, d = [send(sends[k - 1], sign * k, name) for k in (2, 1, 3)]
    return [b, c, d]


def all_z(a, name):
    return by_distance(send_z, [a] * 3, name)


def all_x(a, name):
    return by_distance(send_x, [a] * 3, name)


def all_y(sends, name):
    return by_distance(send_y, sends, name)


def back_z(sends, name):
    return by_distance(send_z, sends, name, -1)


def back_x(sends, name):
    return by_distance(send_x, sends, name, -1)


def up_kernel(y, mine, theirs, wg, wu, whole, s1, s2, s3, own):
    half = mine.shape[0]
    whole[:half] = mine[...]
    whole[half:] = theirs[...]
    n, f = s1.shape[0], wg.shape[1]
    for k, o in ((1, s1), (2, s2), (3, s3), (0, own)):
        rows = whole[block_at(y[0] + k, n), :]
        o[:, :f] = dot(rows, wg[...], 1, 0).astype(o.dtype)
        o[:, f:] = dot(rows, wu[...], 1, 0).astype(o.dtype)


def back_kernel(y, mine, theirs, wd, whole, s1, s2, s3, own):
    half = mine.shape[0]
    whole[:half] = mine[...]
    whole[half:] = theirs[...]
    n = s1.shape[0]
    for k, o in ((1, s1), (2, s2), (3, s3), (0, own)):
        rows = whole[block_at(y[0] + k, n), :]
        o[...] = dot(rows, wd[...], 1, 1).astype(o.dtype)


def sum_y_kernel(own, a, b, c, total, send):
    t = own[...] + a[...].astype(F32) + b[...].astype(F32) + c[...].astype(F32)
    total[...] = t
    send[...] = t.astype(BF)


def hidden_kernel(mine, theirs, out):
    f = out.shape[1]
    gate = mine[:, :f] + theirs[:, :f].astype(F32)
    up = mine[:, f:] + theirs[:, f:].astype(F32)
    out[...] = (gate * jax.nn.sigmoid(gate) * up).astype(BF)


def grads_kernel(mine, theirs, mine_h, theirs_h, out):
    f = mine_h.shape[1]
    gate = mine[:, :f] + theirs[:, :f].astype(F32)
    up = mine[:, f:] + theirs[:, f:].astype(F32)
    gh = mine_h[...] + theirs_h[...].astype(F32)
    sig = jax.nn.sigmoid(gate)
    out[:, :f] = (gh * up * sig * (1.0 + gate * (1.0 - sig))).astype(BF)
    out[:, f:] = (gh * gate * sig).astype(BF)


def place(y, parts, whole):
    n = parts[0].shape[0]
    for k, r in enumerate(parts):
        whole[block_at(y[0] + Y - k, n), :] = r[...]


def out_kernel(y, a, b, c, d, wd, whole, own, theirs):
    place(y, (a, b, c, d), whole)
    half = own.shape[0]
    theirs[...] = dot(whole[half:, :], wd[...], 1, 0).astype(theirs.dtype)
    own[...] = dot(whole[:half, :], wd[...], 1, 0)


def tokens_kernel(y, a, b, c, d, wg, wu, gg, ug, theirs):
    f = gg.shape[1]
    n = a.shape[0]
    for k, r in enumerate((a, b, c, d)):
        at = block_at(y[0] + Y - k, n)
        gg[at, :] = r[:, :f]
        ug[at, :] = r[:, f:]
    half = theirs.shape[0]
    theirs[...] = dot(gg[half:, :], wg[...], 1, 1) + dot(ug[half:, :], wu[...], 1, 1)


def tokens_own_kernel(gg, ug, wg, wu, own):
    half = own.shape[0]
    own[...] = dot(gg[:half, :], wg[...], 1, 1) + dot(ug[:half, :], wu[...], 1, 1)


def rs_first_kernel(mine, theirs, s1, s2, s3, own):
    n = own.shape[0]
    for k, o in enumerate((own, s1, s2, s3)):
        at = slice(k * n, (k + 1) * n)
        o[...] = (mine[at, :] + theirs[at, :].astype(F32)).astype(o.dtype)


def rs_next_kernel(o0, oa, ob, oc, t0, ta, tb, tc, s1, s2, s3, own):
    both = []
    for mine, a, b, c in ((o0, oa, ob, oc), (t0, ta, tb, tc)):
        t = mine[...] + a[...].astype(F32) + b[...].astype(F32)
        both.append(t + c[...].astype(F32))
    n = own.shape[0] // 2
    for k, o in enumerate((own, s1, s2, s3)):
        t = jnp.concatenate([t[k * n : (k + 1) * n] for t in both], axis=0)
        o[...] = t.astype(o.dtype)


def rs_last_kernel(mine, a, b, c, output, grad):
    t = mine[...] + a[...].astype(F32) + b[...].astype(F32) + c[...].astype(F32)
    n = output.shape[0]
    output[...] = t[:n].astype(BF)
    grad[...] = t[n:].astype(BF)


def first_row(own, theirs, after=()):
    rows, w = own.shape
    sends = [((rows // X, w), BF)] * 3 + [((rows // X, w), F32)]
    return call(rs_first_kernel, sends, [own, theirs], after=after)


def on_device(tokens, gate_weight, up_weight, down_weight, cotangent):
    y = lax.rem(lax.axis_index("col"), Y).astype(jnp.int32).reshape(1)
    d, f = gate_weight.shape

    t = gather_z(tokens, all_z(tokens, "tokens_z"))
    g = hold([cotangent], [t])[0]
    g = gather_z(g, all_z(g, "cotangent_z"))
    t = gather_x(t, all_x(t, "tokens_x"), after=[g])
    half = t.shape[0]
    n = CORES * half // Y
    flops = 2 * CORES * half * d * f

    def sends(w):
        return [((CORES * half, d), BF)] + [((n, w), BF)] * 3 + [((n, w), F32)]

    all_tokens, s1, s2, s3, own = call(
        up_kernel, sends(2 * f), [t, send_core(t, "tokens_core"), gate_weight, up_weight], 2 * flops, y
    )
    g = hold([g], [s1])[0]
    got_x = all_x(g, "cotangent_x")
    got = all_y([s1, s2, s3], "gate_up_y")
    g = gather_x(g, got_x, after=got)
    gate_up, part = call(
        sum_y_kernel, [((n, 2 * f), F32), ((n, 2 * f), BF)], [own, *got], after=got_x
    )

    gate_up2 = send_half(part, "gate_up_half")
    all_cotangent, s1, s2, s3, own = call(
        back_kernel, sends(f), [g, send_core(g, "cotangent_core"), down_weight], flops, y
    )
    got = all_y([s1, s2, s3], "hidden_grad_y")
    gh, part = call(
        sum_y_kernel, [((n, f), F32), ((n, f), BF)], [own, *got], after=[gate_up2]
    )
    hidden = call(hidden_kernel, [((n, f), BF)], [gate_up, gate_up2], after=got)[0]

    gh2 = send_half(part, "hidden_grad_half")
    got = all_y([hidden] * 3, "hidden_y")
    all_hidden, own_out, their_out = call(
        out_kernel,
        [((Y * n, f), BF), ((half, d), F32), ((half, d), OUT_CORE)],
        [hidden, *got, down_weight],
        flops,
        y,
        after=[gh2],
    )
    grads = call(
        grads_kernel, [((n, 2 * f), BF)], [gate_up, gate_up2, gh, gh2], after=got
    )[0]

    got = all_y([grads] * 3, "grads_y")
    s1, s2, s3, own_out = first_row(own_out, send_core(their_out, "output_core"))
    got_out = back_x([s1, s2, s3], "output_x")
    gg, ug, their_gt = call(
        tokens_kernel,
        [((Y * n, f), BF), ((Y * n, f), BF), ((half, d), OUT_CORE)],
        [grads, *got, gate_weight, up_weight],
        flops,
        y,
        after=got_out,
    )
    own_gt = call(
        tokens_own_kernel,
        [((half, d), F32)],
        [gg, ug, gate_weight, up_weight],
        flops,
    )[0]

    all_hidden = hold([all_hidden], [their_gt])[0]
    grad_down = dot(all_hidden, all_cotangent, 0, 0).astype(BF)
    their_gt = send_core(their_gt, "token_grad_core")
    s1, s2, s3, own_gt = first_row(own_gt, their_gt, [grad_down])
    got = back_x([s1, s2, s3], "token_grad_x")
    gg, ug = hold([gg, ug], [got[1]])
    grad_gate = dot(all_tokens, gg, 0, 0).astype(BF)
    grad_up = dot(all_tokens, ug, 0, 0).astype(BF)
    rows = tokens.shape[0]
    s1, s2, s3, own = call(
        rs_next_kernel,
        [((2 * rows, d), BF)] * 3 + [((2 * rows, d), F32)],
        [own_out, *got_out, own_gt, *got],
        after=[grad_gate, grad_up],
    )
    got = back_z([s1, s2, s3], "both_z")
    output, grad_tokens = call(rs_last_kernel, [((rows, d), BF)] * 2, [own, *got])
    return (output, grad_tokens, grad_gate, grad_up, grad_down)


OUT_CORE = F32


def solution(mesh):
    return jax.shard_map(
        on_device,
        mesh=mesh,
        in_specs=(
            P("row", "col"),
            P("col", "row"),
            P("col", "row"),
            P("row", "col"),
            P("row", "col"),
        ),
        out_specs=(
            P("row", "col"),
            P("row", "col"),
            P("col", "row"),
            P("col", "row"),
            P("row", "col"),
        ),
        check_vma=False,
    )
```

```python
import jax
import jax.numpy as jnp
from jax import lax
from jax.experimental import pallas as pl
from jax.experimental.pallas import tpu as pltpu
from jax.sharding import PartitionSpec as P

Z, X, CORES, ZH, Y = 4, 4, 2, 2, 4
BF = jnp.bfloat16
F32 = jnp.float32
VMEM_LIMIT = 32 * 1024 * 1024


def row_perm(move):
    pairs = []
    for z in range(Z):
        for x in range(X):
            for c in range(CORES):
                tz, tx, tc = move(z, x, c)
                pairs.append(
                    ((z * X + x) * CORES + c, ((tz % Z) * X + tx % X) * CORES + tc % CORES)
                )
    return pairs


def col_perm(move):
    pairs = []
    for h in range(ZH):
        for y in range(Y):
            th, ty = move(h, y)
            pairs.append((h * Y + y, (th % ZH) * Y + ty % Y))
    return pairs


def send_z(a, k, name):
    with jax.named_scope(name):
        return lax.ppermute(a, "row", row_perm(lambda z, x, c: (z + k, x, c)))


def send_x(a, k, name):
    with jax.named_scope(name):
        return lax.ppermute(a, "row", row_perm(lambda z, x, c: (z, x + k, c)))


def send_core(a, name):
    with jax.named_scope(name):
        return lax.ppermute(a, "row", row_perm(lambda z, x, c: (z, x, c + 1)))


def send_y(a, k, name):
    with jax.named_scope(name):
        return lax.ppermute(a, "col", col_perm(lambda h, y: (h, y + k)))


def send_half(a, name):
    with jax.named_scope(name):
        return lax.ppermute(a, "col", col_perm(lambda h, y: (h + 1, y)))


def dot(left, right, ldim, rdim):
    return lax.dot_general(
        left, right, (((ldim,), (rdim,)), ((), ())), preferred_element_type=F32
    )


def call(kernel, outs, args, flops=0, scalar=None, after=()):
    out_shape = [jax.ShapeDtypeStruct(s, d) for s, d in outs]
    moved = sum(a.size * a.dtype.itemsize for a in args)
    moved += sum(o.size * o.dtype.itemsize for o in out_shape)
    vmem = pl.BlockSpec(memory_space=pltpu.VMEM)
    in_specs = [vmem] * len(args)
    if scalar is not None:
        in_specs = [pl.BlockSpec(memory_space=pltpu.SMEM)] + in_specs
        args = [scalar, *args]
    n = len(args)
    body = kernel
    if after:
        in_specs = in_specs + [pl.BlockSpec(memory_space=pl.ANY)] * len(after)
        args = [*args, *after]

        def body(*refs):
            kernel(*refs[:n], *refs[n + len(after) :])

    return pl.pallas_call(
        body,
        name=kernel.__name__.removesuffix("_kernel"),
        out_shape=out_shape,
        in_specs=in_specs,
        out_specs=[vmem] * len(outs),
        compiler_params=pltpu.CompilerParams(vmem_limit_bytes=VMEM_LIMIT),
        cost_estimate=pl.CostEstimate(
            flops=flops, bytes_accessed=moved, transcendentals=0
        ),
    )(*args)


def block_at(index, size):
    return pl.ds(pl.multiple_of(lax.rem(index, Y) * size, size), size)


def cat_z_kernel(a, b, c, d, out):
    parts = [r[...].astype(F32) for r in (a, b, c, d)]
    out[...] = jnp.concatenate(parts, axis=0).astype(BF)


def cat_x_kernel(a, b, c, d, out):
    size = a.shape[0]
    for k, r in enumerate((a, b, c, d)):
        out[k * size : (k + 1) * size] = r[...]


def hold_kernel(*refs):
    half = len(refs) // 2
    for src, dst in zip(refs[:half], refs[half:]):
        dst[...] = src[...]


def hold(args, after):
    return call(hold_kernel, [(a.shape, a.dtype) for a in args], list(args), after=after)


def gather_z(a, got):
    n, w = a.shape
    own = hold([a], [])[0]
    return call(cat_z_kernel, [((Z * n, w), BF)], [own, *got])[0]


def gather_x(a, got, after=()):
    n, w = a.shape
    return call(cat_x_kernel, [((X * n, w), BF)], [a, *got], after=after)[0]


def by_distance(send, sends, name, sign=1):
    c, b, d = [send(sends[k - 1], sign * k, name) for k in (2, 1, 3)]
    return [b, c, d]


def all_z(a, name):
    return by_distance(send_z, [a] * 3, name)


def all_x(a, name):
    return by_distance(send_x, [a] * 3, name)


def all_y(sends, name):
    return by_distance(send_y, sends, name)


def back_z(sends, name):
    return by_distance(send_z, sends, name, -1)


def back_x(sends, name):
    return by_distance(send_x, sends, name, -1)


def up_kernel(y, mine, theirs, wg, wu, whole, s1, s2, s3, own):
    half = mine.shape[0]
    whole[:half] = mine[...]
    whole[half:] = theirs[...]
    n, f = s1.shape[0], wg.shape[1]
    for k, o in ((1, s1), (2, s2), (3, s3), (0, own)):
        rows = whole[block_at(y[0] + k, n), :]
        o[:, :f] = dot(rows, wg[...], 1, 0).astype(o.dtype)
        o[:, f:] = dot(rows, wu[...], 1, 0).astype(o.dtype)


def back_kernel(y, mine, theirs, wd, whole, s1, s2, s3, own):
    half = mine.shape[0]
    whole[:half] = mine[...]
    whole[half:] = theirs[...]
    n = s1.shape[0]
    for k, o in ((1, s1), (2, s2), (3, s3), (0, own)):
        rows = whole[block_at(y[0] + k, n), :]
        o[...] = dot(rows, wd[...], 1, 1).astype(o.dtype)


def sum_y_kernel(own, a, b, c, total, send):
    t = own[...] + a[...].astype(F32) + b[...].astype(F32) + c[...].astype(F32)
    total[...] = t
    send[...] = t.astype(BF)


def hidden_kernel(mine, theirs, out):
    f = out.shape[1]
    gate = mine[:, :f] + theirs[:, :f].astype(F32)
    up = mine[:, f:] + theirs[:, f:].astype(F32)
    out[...] = (gate * jax.nn.sigmoid(gate) * up).astype(BF)


def grads_kernel(mine, theirs, mine_h, theirs_h, out):
    f = mine_h.shape[1]
    gate = mine[:, :f] + theirs[:, :f].astype(F32)
    up = mine[:, f:] + theirs[:, f:].astype(F32)
    gh = mine_h[...] + theirs_h[...].astype(F32)
    sig = jax.nn.sigmoid(gate)
    out[:, :f] = (gh * up * sig * (1.0 + gate * (1.0 - sig))).astype(BF)
    out[:, f:] = (gh * gate * sig).astype(BF)


def place(y, parts, whole):
    n = parts[0].shape[0]
    for k, r in enumerate(parts):
        whole[block_at(y[0] + Y - k, n), :] = r[...]


def out_kernel(y, a, b, c, d, wd, whole, own, theirs):
    place(y, (a, b, c, d), whole)
    half = own.shape[0]
    theirs[...] = dot(whole[half:, :], wd[...], 1, 0).astype(theirs.dtype)
    own[...] = dot(whole[:half, :], wd[...], 1, 0)


def tokens_kernel(y, a, b, c, d, wg, wu, gg, ug, theirs):
    f = gg.shape[1]
    n = a.shape[0]
    for k, r in enumerate((a, b, c, d)):
        at = block_at(y[0] + Y - k, n)
        gg[at, :] = r[:, :f]
        ug[at, :] = r[:, f:]
    half = theirs.shape[0]
    theirs[...] = dot(gg[half:, :], wg[...], 1, 1) + dot(ug[half:, :], wu[...], 1, 1)


TILE = 256


def token_products(first, gg, ug, wg, wu, o):
    rows = slice(first, first + o.shape[0])

    @pl.loop(0, o.shape[1] // TILE)
    def _(j):
        at = pl.ds(pl.multiple_of(j * TILE, TILE), TILE)
        t = dot(gg[rows, :], wg[at, :], 1, 1)
        o[:, at] = t + dot(ug[rows, :], wu[at, :], 1, 1)


def tokens_own_kernel(gg, ug, wg, wu, own):
    token_products(0, gg, ug, wg, wu, own)


def rs_first_kernel(mine, theirs, s1, s2, s3, own):
    n = own.shape[0]
    for k, o in enumerate((own, s1, s2, s3)):
        at = slice(k * n, (k + 1) * n)
        o[...] = (mine[at, :] + theirs[at, :].astype(F32)).astype(o.dtype)


def rs_next_kernel(mine, a, b, c, s1, s2, s3, own):
    n = own.shape[0]
    t = mine[...] + a[...].astype(F32) + b[...].astype(F32) + c[...].astype(F32)
    for k, o in enumerate((own, s1, s2, s3)):
        o[...] = t[k * n : (k + 1) * n].astype(o.dtype)


def rs_last_kernel(mine, a, b, c, out):
    t = mine[...] + a[...].astype(F32) + b[...].astype(F32) + c[...].astype(F32)
    out[...] = t.astype(BF)


def next_row(own, got, after=()):
    rows, w = own.shape
    sends = [((rows // Z, w), BF)] * 3 + [((rows // Z, w), F32)]
    return call(rs_next_kernel, sends, [own, *got], after=after)


def last_row(own, got):
    return call(rs_last_kernel, [(own.shape, BF)], [own, *got])[0]


def first_row(own, theirs, after=()):
    rows, w = own.shape
    sends = [((rows // X, w), BF)] * 3 + [((rows // X, w), F32)]
    return call(rs_first_kernel, sends, [own, theirs], after=after)


def on_device(tokens, gate_weight, up_weight, down_weight, cotangent):
    y = lax.rem(lax.axis_index("col"), Y).astype(jnp.int32).reshape(1)
    d, f = gate_weight.shape

    t = gather_z(tokens, all_z(tokens, "tokens_z"))
    g = hold([cotangent], [t])[0]
    got = all_z(g, "cotangent_z")
    g = gather_z(g, got)
    t = gather_x(t, all_x(t, "tokens_x"), after=got[:2])
    half = t.shape[0]
    n = CORES * half // Y
    flops = 2 * CORES * half * d * f

    def sends(w):
        return [((CORES * half, d), BF)] + [((n, w), BF)] * 3 + [((n, w), F32)]

    all_tokens, s1, s2, s3, own = call(
        up_kernel, sends(2 * f), [t, send_core(t, "tokens_core"), gate_weight, up_weight], 2 * flops, y
    )
    g = hold([g], [s1])[0]
    got_x = all_x(g, "cotangent_x")
    got = all_y([s1, s2, s3], "gate_up_y")
    g = gather_x(g, got_x, after=got)
    gate_up, part = call(
        sum_y_kernel, [((n, 2 * f), F32), ((n, 2 * f), BF)], [own, *got], after=got_x
    )

    gate_up2 = send_half(part, "gate_up_half")
    all_cotangent, s1, s2, s3, own = call(
        back_kernel, sends(f), [g, send_core(g, "cotangent_core"), down_weight], flops, y
    )
    got = all_y([s1, s2, s3], "hidden_grad_y")
    gh, part = call(
        sum_y_kernel, [((n, f), F32), ((n, f), BF)], [own, *got], after=[gate_up2]
    )
    hidden = call(hidden_kernel, [((n, f), BF)], [gate_up, gate_up2], after=got)[0]

    gh2 = send_half(part, "hidden_grad_half")
    got = all_y([hidden] * 3, "hidden_y")
    all_hidden, own_out, their_out = call(
        out_kernel,
        [((Y * n, f), BF), ((half, d), F32), ((half, d), OUT_CORE)],
        [hidden, *got, down_weight],
        flops,
        y,
        after=[gh2],
    )
    grads = call(
        grads_kernel, [((n, 2 * f), BF)], [gate_up, gate_up2, gh, gh2], after=got
    )[0]

    got = all_y([grads] * 3, "grads_y")
    s1, s2, s3, own_out = first_row(own_out, send_core(their_out, "output_core"))
    got_out = back_x([s1, s2, s3], "output_x")
    gg, ug, their_gt = call(
        tokens_kernel,
        [((Y * n, f), BF), ((Y * n, f), BF), ((half, d), OUT_CORE)],
        [grads, *got, gate_weight, up_weight],
        flops,
        y,
        after=got_out,
    )
    own_gt = call(
        tokens_own_kernel,
        [((half, d), F32)],
        [gg, ug, gate_weight, up_weight],
        flops,
    )[0]

    all_hidden = hold([all_hidden], [their_gt])[0]
    grad_down = dot(all_hidden, all_cotangent, 0, 0).astype(BF)
    s1, s2, s3, own_out = next_row(own_out, got_out)
    their_gt = send_core(their_gt, "token_grad_core")
    t1, t2, t3, own_gt = first_row(own_gt, their_gt, [grad_down, s1])
    got = back_x([t1, t2, t3], "token_grad_x")
    got_out = back_z(hold([s1, s2, s3], [got[1]]), "output_z")
    gg, ug = hold([gg, ug], [got[1]])
    grad_gate = dot(all_tokens, gg, 0, 0).astype(BF)
    grad_up = dot(all_tokens, ug, 0, 0).astype(BF)
    s1, s2, s3, own_gt = next_row(own_gt, got, after=[grad_gate, grad_up, got_out[1]])
    got = back_z([s1, s2, s3], "token_grad_z")
    grad_tokens = last_row(own_gt, got)
    output = last_row(own_out, got_out)
    return (output, grad_tokens, grad_gate, grad_up, grad_down)


OUT_CORE = F32


def solution(mesh):
    return jax.shard_map(
        on_device,
        mesh=mesh,
        in_specs=(
            P("row", "col"),
            P("col", "row"),
            P("col", "row"),
            P("row", "col"),
            P("row", "col"),
        ),
        out_specs=(
            P("row", "col"),
            P("row", "col"),
            P("col", "row"),
            P("col", "row"),
            P("row", "col"),
        ),
        check_vma=False,
    )
```

```python
import jax
import jax.numpy as jnp
from jax import lax
from jax.experimental import pallas as pl
from jax.experimental.pallas import tpu as pltpu
from jax.sharding import PartitionSpec as P

Z, X, CORES, ZH, Y = 4, 4, 2, 2, 4
BF = jnp.bfloat16
F32 = jnp.float32
VMEM_LIMIT = 32 * 1024 * 1024


def row_perm(move):
    pairs = []
    for z in range(Z):
        for x in range(X):
            for c in range(CORES):
                tz, tx, tc = move(z, x, c)
                pairs.append(
                    ((z * X + x) * CORES + c, ((tz % Z) * X + tx % X) * CORES + tc % CORES)
                )
    return pairs


def col_perm(move):
    pairs = []
    for h in range(ZH):
        for y in range(Y):
            th, ty = move(h, y)
            pairs.append((h * Y + y, (th % ZH) * Y + ty % Y))
    return pairs


def send_z(a, k, name):
    with jax.named_scope(name):
        return lax.ppermute(a, "row", row_perm(lambda z, x, c: (z + k, x, c)))


def send_x(a, k, name):
    with jax.named_scope(name):
        return lax.ppermute(a, "row", row_perm(lambda z, x, c: (z, x + k, c)))


def send_core(a, name):
    with jax.named_scope(name):
        return lax.ppermute(a, "row", row_perm(lambda z, x, c: (z, x, c + 1)))


def send_y(a, k, name):
    with jax.named_scope(name):
        return lax.ppermute(a, "col", col_perm(lambda h, y: (h, y + k)))


def send_half(a, name):
    with jax.named_scope(name):
        return lax.ppermute(a, "col", col_perm(lambda h, y: (h + 1, y)))


def dot(left, right, ldim, rdim):
    return lax.dot_general(
        left, right, (((ldim,), (rdim,)), ((), ())), preferred_element_type=F32
    )


def call(kernel, outs, args, flops=0, scalar=None, after=()):
    out_shape = [jax.ShapeDtypeStruct(s, d) for s, d in outs]
    moved = sum(a.size * a.dtype.itemsize for a in args)
    moved += sum(o.size * o.dtype.itemsize for o in out_shape)
    vmem = pl.BlockSpec(memory_space=pltpu.VMEM)
    in_specs = [vmem] * len(args)
    if scalar is not None:
        in_specs = [pl.BlockSpec(memory_space=pltpu.SMEM)] + in_specs
        args = [scalar, *args]
    n = len(args)
    body = kernel
    if after:
        in_specs = in_specs + [pl.BlockSpec(memory_space=pl.ANY)] * len(after)
        args = [*args, *after]

        def body(*refs):
            kernel(*refs[:n], *refs[n + len(after) :])

    return pl.pallas_call(
        body,
        name=kernel.__name__.removesuffix("_kernel"),
        out_shape=out_shape,
        in_specs=in_specs,
        out_specs=[vmem] * len(outs),
        compiler_params=pltpu.CompilerParams(vmem_limit_bytes=VMEM_LIMIT),
        cost_estimate=pl.CostEstimate(
            flops=flops, bytes_accessed=moved, transcendentals=0
        ),
    )(*args)


def block_at(index, size):
    return pl.ds(pl.multiple_of(lax.rem(index, Y) * size, size), size)


def cat_z_kernel(a, b, c, d, out):
    parts = [r[...].astype(F32) for r in (a, b, c, d)]
    out[...] = jnp.concatenate(parts, axis=0).astype(BF)


def cat_x_kernel(a, b, c, d, out):
    size = a.shape[0]
    for k, r in enumerate((a, b, c, d)):
        out[k * size : (k + 1) * size] = r[...]


def hold_kernel(*refs):
    half = len(refs) // 2
    for src, dst in zip(refs[:half], refs[half:]):
        dst[...] = src[...]


def hold(args, after):
    return call(hold_kernel, [(a.shape, a.dtype) for a in args], list(args), after=after)


def gather_z(a, got):
    n, w = a.shape
    own = hold([a], [])[0]
    return call(cat_z_kernel, [((Z * n, w), BF)], [own, *got])[0]


def gather_x(a, got, after=()):
    n, w = a.shape
    return call(cat_x_kernel, [((X * n, w), BF)], [a, *got], after=after)[0]


def by_distance(send, sends, name, sign=1):
    c, b, d = [send(sends[k - 1], sign * k, name) for k in (2, 1, 3)]
    return [b, c, d]


def all_z(a, name):
    return by_distance(send_z, [a] * 3, name)


def all_x(a, name):
    return by_distance(send_x, [a] * 3, name)


def all_y(sends, name):
    return by_distance(send_y, sends, name)


def back_z(sends, name):
    return by_distance(send_z, sends, name, -1)


def back_x(sends, name):
    return by_distance(send_x, sends, name, -1)


def up_kernel(y, mine, theirs, wg, wu, whole, s1, s2, s3, own):
    half = mine.shape[0]
    whole[:half] = mine[...]
    whole[half:] = theirs[...]
    n, f = s1.shape[0], wg.shape[1]
    for k, o in ((1, s1), (2, s2), (3, s3), (0, own)):
        rows = whole[block_at(y[0] + k, n), :]
        o[:, :f] = dot(rows, wg[...], 1, 0).astype(o.dtype)
        o[:, f:] = dot(rows, wu[...], 1, 0).astype(o.dtype)


def back_kernel(y, mine, theirs, wd, whole, s1, s2, s3, own):
    half = mine.shape[0]
    whole[:half] = mine[...]
    whole[half:] = theirs[...]
    n = s1.shape[0]
    for k, o in ((1, s1), (2, s2), (3, s3), (0, own)):
        rows = whole[block_at(y[0] + k, n), :]
        o[...] = dot(rows, wd[...], 1, 1).astype(o.dtype)


def sum_y_kernel(own, a, b, c, total, send):
    t = own[...] + a[...].astype(F32) + b[...].astype(F32) + c[...].astype(F32)
    total[...] = t
    send[...] = t.astype(BF)


def hidden_kernel(mine, theirs, out):
    f = out.shape[1]
    gate = mine[:, :f] + theirs[:, :f].astype(F32)
    up = mine[:, f:] + theirs[:, f:].astype(F32)
    out[...] = (gate * jax.nn.sigmoid(gate) * up).astype(BF)


def grads_kernel(mine, theirs, mine_h, theirs_h, out):
    f = mine_h.shape[1]
    gate = mine[:, :f] + theirs[:, :f].astype(F32)
    up = mine[:, f:] + theirs[:, f:].astype(F32)
    gh = mine_h[...] + theirs_h[...].astype(F32)
    sig = jax.nn.sigmoid(gate)
    out[:, :f] = (gh * up * sig * (1.0 + gate * (1.0 - sig))).astype(BF)
    out[:, f:] = (gh * gate * sig).astype(BF)


def place(y, parts, whole):
    n = parts[0].shape[0]
    for k, r in enumerate(parts):
        whole[block_at(y[0] + Y - k, n), :] = r[...]


def out_kernel(y, a, b, c, d, wd, whole, own, theirs):
    place(y, (a, b, c, d), whole)
    half = own.shape[0]
    theirs[...] = dot(whole[half:, :], wd[...], 1, 0).astype(theirs.dtype)
    own[...] = dot(whole[:half, :], wd[...], 1, 0)


def tokens_kernel(y, a, b, c, d, wg, wu, gg, ug, theirs):
    f = gg.shape[1]
    n = a.shape[0]
    for k, r in enumerate((a, b, c, d)):
        at = block_at(y[0] + Y - k, n)
        gg[at, :] = r[:, :f]
        ug[at, :] = r[:, f:]
    half = theirs.shape[0]
    theirs[...] = dot(gg[half:, :], wg[...], 1, 1) + dot(ug[half:, :], wu[...], 1, 1)


TILE = 256


def token_products(first, gg, ug, wg, wu, o):
    rows = slice(first, first + o.shape[0])

    @pl.loop(0, o.shape[1] // TILE)
    def _(j):
        at = pl.ds(pl.multiple_of(j * TILE, TILE), TILE)
        t = dot(gg[rows, :], wg[at, :], 1, 1)
        o[:, at] = t + dot(ug[rows, :], wu[at, :], 1, 1)


def tokens_own_kernel(gg, ug, wg, wu, own):
    token_products(0, gg, ug, wg, wu, own)


def rs_first_kernel(mine, theirs, s1, s2, s3, own):
    n = own.shape[0]
    for k, o in enumerate((own, s1, s2, s3)):
        at = slice(k * n, (k + 1) * n)
        o[...] = (mine[at, :] + theirs[at, :].astype(F32)).astype(o.dtype)


def rs_next_kernel(mine, a, b, c, s1, s2, s3, own):
    n = own.shape[0]
    t = mine[...] + a[...].astype(F32) + b[...].astype(F32) + c[...].astype(F32)
    for k, o in enumerate((own, s1, s2, s3)):
        o[...] = t[k * n : (k + 1) * n].astype(o.dtype)


def rs_last_kernel(mine, a, b, c, out):
    t = mine[...] + a[...].astype(F32) + b[...].astype(F32) + c[...].astype(F32)
    out[...] = t.astype(BF)


def next_row(own, got, after=()):
    rows, w = own.shape
    sends = [((rows // Z, w), BF)] * 3 + [((rows // Z, w), F32)]
    return call(rs_next_kernel, sends, [own, *got], after=after)


def last_row(own, got):
    return call(rs_last_kernel, [(own.shape, BF)], [own, *got])[0]


def first_row(own, theirs, after=()):
    rows, w = own.shape
    sends = [((rows // X, w), BF)] * 3 + [((rows // X, w), F32)]
    return call(rs_first_kernel, sends, [own, theirs], after=after)


def on_device(tokens, gate_weight, up_weight, down_weight, cotangent):
    y = lax.rem(lax.axis_index("col"), Y).astype(jnp.int32).reshape(1)
    d, f = gate_weight.shape

    t = gather_z(tokens, all_z(tokens, "tokens_z"))
    g = hold([cotangent], [t])[0]
    got = all_z(g, "cotangent_z")
    g = gather_z(g, got)
    t = gather_x(t, all_x(t, "tokens_x"), after=got[:2])
    half = t.shape[0]
    n = CORES * half // Y
    flops = 2 * CORES * half * d * f

    def sends(w):
        return [((CORES * half, d), BF)] + [((n, w), BF)] * 3 + [((n, w), F32)]

    all_tokens, s1, s2, s3, own = call(
        up_kernel, sends(2 * f), [t, send_core(t, "tokens_core"), gate_weight, up_weight], 2 * flops, y
    )
    g = hold([g], [s1])[0]
    got_x = all_x(g, "cotangent_x")
    got = all_y([s1, s2, s3], "gate_up_y")
    g = gather_x(g, got_x, after=got)
    gate_up, part = call(
        sum_y_kernel, [((n, 2 * f), F32), ((n, 2 * f), BF)], [own, *got], after=got_x
    )

    gate_up2 = send_half(part, "gate_up_half")
    all_cotangent, s1, s2, s3, own = call(
        back_kernel, sends(f), [g, send_core(g, "cotangent_core"), down_weight], flops, y
    )
    got = all_y([s1, s2, s3], "hidden_grad_y")
    gh, part = call(
        sum_y_kernel, [((n, f), F32), ((n, f), BF)], [own, *got], after=[gate_up2]
    )
    hidden = call(hidden_kernel, [((n, f), BF)], [gate_up, gate_up2], after=got)[0]

    gh2 = send_half(part, "hidden_grad_half")
    got = all_y([hidden] * 3, "hidden_y")
    grads = call(
        grads_kernel, [((n, 2 * f), BF)], [gate_up, gate_up2, gh, gh2], after=got
    )[0]
    all_hidden, own_out, their_out = call(
        out_kernel,
        [((Y * n, f), BF), ((half, d), F32), ((half, d), OUT_CORE)],
        [hidden, *got, down_weight],
        flops,
        y,
        after=[gh2, grads],
    )

    got = all_y([grads] * 3, "grads_y")
    s1, s2, s3, own_out = first_row(own_out, send_core(their_out, "output_core"))
    got_out = back_x([s1, s2, s3], "output_x")
    gg, ug, their_gt = call(
        tokens_kernel,
        [((Y * n, f), BF), ((Y * n, f), BF), ((half, d), OUT_CORE)],
        [grads, *got, gate_weight, up_weight],
        flops,
        y,
        after=got_out,
    )
    own_gt = call(
        tokens_own_kernel,
        [((half, d), F32)],
        [gg, ug, gate_weight, up_weight],
        flops,
    )[0]

    all_hidden = hold([all_hidden], [their_gt])[0]
    grad_down = dot(all_hidden, all_cotangent, 0, 0).astype(BF)
    s1, s2, s3, own_out = next_row(own_out, got_out)
    their_gt = send_core(their_gt, "token_grad_core")
    t1, t2, t3, own_gt = first_row(own_gt, their_gt, [grad_down, s1])
    got = back_x([t1, t2, t3], "token_grad_x")
    got_out = back_z(hold([s1, s2, s3], [got[1]]), "output_z")
    gg, ug = hold([gg, ug], [got[1]])
    grad_gate = dot(all_tokens, gg, 0, 0).astype(BF)
    grad_up = dot(all_tokens, ug, 0, 0).astype(BF)
    s1, s2, s3, own_gt = next_row(own_gt, got, after=[grad_gate, grad_up, got_out[1]])
    got = back_z([s1, s2, s3], "token_grad_z")
    grad_tokens = last_row(own_gt, got)
    output = last_row(own_out, got_out)
    return (output, grad_tokens, grad_gate, grad_up, grad_down)


OUT_CORE = F32


def solution(mesh):
    return jax.shard_map(
        on_device,
        mesh=mesh,
        in_specs=(
            P("row", "col"),
            P("col", "row"),
            P("col", "row"),
            P("row", "col"),
            P("row", "col"),
        ),
        out_specs=(
            P("row", "col"),
            P("row", "col"),
            P("col", "row"),
            P("col", "row"),
            P("row", "col"),
        ),
        check_vma=False,
    )
```
